32 devices in a mesh: row: 4 (over y, x), col: 8 (over z, core).
Axes of the slice: x: 2, y: 2, z: 4, core: 2. Of those that a mesh axis runs over, the one named last changes fastest.
Arguments:
- member_outputs: float32 [3, 8192, 512], P(None, ('row', 'col')), may hold values from -6 to 6
- pivot_inverse_matrices: bfloat16 [2, 8192, 8192], P(None, 'col', 'row'), may hold values from -1 to 1.25, as said below
- former_subdiagonal_tiles: bfloat16 [2, 8192, 8192], P(None, 'row', 'col'), may hold values from -0.09375 to 0.09375
- latter_subdiagonal_tiles: bfloat16 [1, 8192, 8192], P(None, 'row', 'col'), may hold values from -0.09375 to 0.09375
Outputs:
- whitened: bfloat16 [2, 8192, 512], P(None, 'col')
- trailing: float32 [1, 8192, 512], P(None, ('row', 'col'))
- projections: float32 [256, 512], replicated
The draws below stay inside these ranges and needn't reach their ends.
Inputs may be any that keep to these rules, and one draw needn't show every extreme that they name: `pivot_inverse_matrices`: each block is lower triangular with a positive diagonal: the inverse of a diagonal block of the error covariance's Cholesky factor.
All inputs are finite; a program needn't handle non-finite values.
Results may differ from the reference program's by a relative error of at most 0.0057.
Values may be sent and summed in bfloat16 or wider, within the bound.
A program may use at most 64 MiB of HBM per device.

```python
import jax
import jax.numpy as jnp
from jax import lax

MEASURES_PER_TILE = 8192
MEMBER_NUMBER = 256
SPAN_TILE_NUMBER = 3


def draw_pivot_inverse_matrices(key, part):
    key_off = jax.random.fold_in(key, 11)
    key_diag = jax.random.fold_in(key, 12)
    entries = jnp.clip(jax.random.normal(key_off, (2, MEASURES_PER_TILE, MEASURES_PER_TILE), jnp.float32), -6.0, 6.0)
    diagonal = 0.8 + 0.4 * jax.random.uniform(key_diag, (2, MEASURES_PER_TILE, 1), jnp.float32)
    row_index = lax.broadcasted_iota(jnp.int32, (MEASURES_PER_TILE, MEASURES_PER_TILE), 0)
    col_index = lax.broadcasted_iota(jnp.int32, (MEASURES_PER_TILE, MEASURES_PER_TILE), 1)
    lower = (col_index < row_index).astype(jnp.float32)
    identity = (col_index == row_index).astype(jnp.float32)
    values = entries * lower * (0.7 / jnp.sqrt(jnp.float32(MEASURES_PER_TILE))) + identity * diagonal
    return values.astype(jnp.bfloat16)


def with_spikes(array, rng, source, target, shards_of, factor):
    def block_of(position):
        return (jnp.arange(array.shape[position]) // (array.shape[position] // shards_of)).reshape((-1,) + (1,) * (array.ndim - 1 - position))

    near = jax.random.permutation(rng, shards_of)[block_of(target)]
    far = (block_of(target) + shards_of // 2) % shards_of
    return jnp.where((block_of(source) == near) | (block_of(source) == far), factor * array, array)


def levels(stream_key, dims, shards, low, high):
    gain, own = 1.0, jax.random.fold_in(stream_key, 6)
    for dim, shards_of in shards:
        heights = jnp.exp(jax.random.uniform(jax.random.fold_in(own, dim), (shards_of,), jnp.float32, low / len(shards), high / len(shards)))
        gain = gain * jnp.repeat(heights, dims[dim] // shards_of).reshape([-1 if axis == dim else 1 for axis in range(len(dims))])
    return gain


def normal_values(own_key, extent, scale, reach, pieces=(), dtype=jnp.bfloat16):
    array = scale * jax.random.normal(own_key, extent, jnp.float32)
    if pieces:
        array = array * levels(own_key, extent, pieces, -0.22, 0.18)
    return jnp.clip(array, -reach, reach).astype(dtype)


def bell_draw_with(stream_key, dims, width, limit, split, heavy, held_as=jnp.bfloat16):
    drawn = width * jax.random.normal(stream_key, dims, jnp.float32)
    if split:
        drawn = drawn * levels(stream_key, dims, split, -0.22, 0.18)
    return jnp.clip(with_spikes(drawn, jax.random.fold_in(stream_key, 3), *heavy), -limit, limit).astype(held_as)


def setup_inputs(seed: int = 0) -> dict:
    keys = jax.random.split(jax.random.key(seed), 5)
    member_outputs = normal_values(keys[0], (SPAN_TILE_NUMBER, MEASURES_PER_TILE, 2 * MEMBER_NUMBER), 1.0, 6.0, ((1, 32),), jnp.float32)
    pivot_inverse_matrices = draw_pivot_inverse_matrices(jax.random.fold_in(keys[4], 71), 0)
    former_subdiagonal_tiles = bell_draw_with(keys[2], (SPAN_TILE_NUMBER - 1, MEASURES_PER_TILE, MEASURES_PER_TILE), MEASURES_PER_TILE ** -0.5, 0.09375, ((1, 4), (2, 8)), (2, 1, 8, 2.0))
    latter_subdiagonal_tiles = bell_draw_with(keys[3], (SPAN_TILE_NUMBER - 2, MEASURES_PER_TILE, MEASURES_PER_TILE), MEASURES_PER_TILE ** -0.5, 0.09375, ((1, 4), (2, 8)), (2, 1, 8, 2.0))
    return {"member_outputs": member_outputs, "pivot_inverse_matrices": pivot_inverse_matrices, "former_subdiagonal_tiles": former_subdiagonal_tiles, "latter_subdiagonal_tiles": latter_subdiagonal_tiles}


def stripe_aggregate(panel_tiles, white_bf):
    def one_tile(tile):
        return jnp.dot(tile, white_bf, preferred_element_type=jnp.float32)
    return lax.map(one_tile, panel_tiles)


def reference(member_outputs, pivot_inverse_matrices, former_subdiagonal_tiles, latter_subdiagonal_tiles):
    initial_clipped_factor = member_outputs[0].astype(jnp.bfloat16)
    white_first = jnp.dot(pivot_inverse_matrices[0], initial_clipped_factor, preferred_element_type=jnp.float32)
    starting_cheap_cholesky = white_first.astype(jnp.bfloat16)
    fresh_strip_entries = member_outputs[1:] - stripe_aggregate(former_subdiagonal_tiles, starting_cheap_cholesky)
    second_rounded = fresh_strip_entries[0].astype(jnp.bfloat16)
    white_second = jnp.dot(pivot_inverse_matrices[1], second_rounded, preferred_element_type=jnp.float32)
    later_narrow_piece = white_second.astype(jnp.bfloat16)
    trailing = fresh_strip_entries[1:] - stripe_aggregate(latter_subdiagonal_tiles, later_narrow_piece)
    whitened = jnp.stack([starting_cheap_cholesky, later_narrow_piece])
    projections = jnp.dot(starting_cheap_cholesky[:, :MEMBER_NUMBER].T, starting_cheap_cholesky, preferred_element_type=jnp.float32)
    projections = projections + jnp.dot(later_narrow_piece[:, :MEMBER_NUMBER].T, later_narrow_piece, preferred_element_type=jnp.float32)
    return whitened, trailing, projections
```

```python
import functools

import jax
import jax.numpy as jnp
from jax import lax
from jax.experimental import pallas as pl
from jax.experimental.pallas import tpu as pltpu
from jax.sharding import PartitionSpec as P

MESH = pl.DeviceIdType.MESH
BF = jnp.bfloat16
F32 = jnp.float32
CHUNKS = 2


def kernel(
    R, Z, b, n, e,
    m_h, p_h, f_h, l_h,
    wh_out, tr_out, pr_out,
    m_v, p_v, f_v, l_v, xg, rs_s, rs_r, wv, acc, acc2, ps_s, ps_r, zs_s, zs_r, tr_v,
    pacc, pp_r, pz, pg,
    ld_sem, out_sem, po_sem,
    xz_s, xz_r, xp_s, xp_r, ra_s, ra_r, rb_s, rb_r, pa_s, pa_r, za_s, za_r,
    q_s, q_r, qz_s, qz_r, qr_s, qr_r,
):
    r = lax.axis_index("row")
    c = lax.axis_index("col")
    z = lax.div(c, 2)
    k = lax.rem(c, 2)
    rb, kb = R * b, 2 * Z * b
    partner = (r, z * 2 + 1 - k)

    def zpeer(zz):
        return (r, zz * 2 + k)

    def zz_of(d):
        return lax.rem(z + d, Z)

    def rr_of(d):
        return lax.rem(r + d, R)

    def rows(block, size, count=None):
        return pl.ds(pl.multiple_of(block * size, size), size if count is None else count)

    loads = {}

    def load(name, index, src, dst):
        copy = pltpu.make_async_copy(src, dst, ld_sem.at[index])
        copy.start()
        loads[name] = copy

    load("m", 0, m_h, m_v)
    load("p0", 1, p_h.at[0], p_v.at[0])
    load("f0", 2, f_h.at[0], f_v.at[0])
    load("p1", 3, p_h.at[1], p_v.at[1])
    load("f1", 4, f_h.at[1], f_v.at[1])
    load("l", 5, l_h.at[0], l_v.at[0])

    barrier = pltpu.get_barrier_semaphore()
    peers = [partner] + [zpeer(zz_of(d)) for d in range(1, Z)]
    peers += [(rr_of(d), c) for d in range(1, R)]
    for peer in peers:
        pl.semaphore_signal(barrier, inc=1, device_id=peer, device_id_type=MESH)
    pl.semaphore_wait(barrier, len(peers))

    sends = []
    local = []

    def send(src, dst, ssem, rsem, device):
        copy = pltpu.make_async_remote_copy(
            src_ref=src, dst_ref=dst, send_sem=ssem, recv_sem=rsem,
            device_id=device, device_id_type=MESH,
        )
        copy.start()
        sends.append(copy)

    def arrived(dst, ssem, rsem):
        pltpu.make_async_remote_copy(
            src_ref=dst, dst_ref=dst, send_sem=ssem, recv_sem=rsem,
            device_id=partner, device_id_type=MESH,
        ).wait_recv()

    waited = set()

    def ready(name):
        if name not in waited:
            waited.add(name)
            loads[name].wait()

    def matmul(a, x, total, put):
        tile = min(512, total)

        def step(i, carry):
            at = pl.ds(pl.multiple_of(i * tile, tile), tile)
            put(at, jnp.dot(a[at, :], x[...], preferred_element_type=F32))
            return carry

        lax.fori_loop(0, total // tile, step, 0)

    def xblock(s, j, cc):
        return xg.at[s, j, rows(cc, b), :]

    def give_x(s, j):
        mine = xblock(s, j, c)
        for d in range(1, Z):
            send(mine, mine, xz_s.at[s, j, d], xz_r.at[s, j, z], zpeer(zz_of(d)))
        send(mine, mine, xp_s.at[s, j, z], xp_r.at[s, j, z], partner)

    def p0(j):
        xg[0, j, rows(c, b), :] = m_v[0, :, j * n:(j + 1) * n].astype(BF)
        give_x(0, j)

    def p1(s, j):
        for d in range(1, Z):
            zz = zz_of(d)
            blk = xblock(s, j, zz * 2 + k)
            arrived(blk, xz_s.at[s, j, d], xz_r.at[s, j, zz])
            send(blk, blk, xp_s.at[s, j, zz], xp_r.at[s, j, zz], partner)

    def p2(s, j):
        for d in range(Z):
            zz = zz_of(d)
            arrived(xblock(s, j, zz * 2 + 1 - k), xp_s.at[s, j, zz], xp_r.at[s, j, zz])
        ready("p%d" % s)

        def put(at, value):
            acc[j, at, :] = value
            rs_s[s, j, at, :] = value.astype(BF)

        matmul(p_v.at[s], xg.at[s, j], rb, put)
        for d in range(1, R):
            rr = rr_of(d)
            send(rs_s.at[s, j, rows(rr, b), :], rs_r.at[s, j, r],
                 ra_s.at[s, j, d], ra_r.at[s, j, r], (rr, c))

    def p3(s, j):
        total = acc[j, rows(r, b), :]
        for d in range(1, R):
            rr = rr_of(d)
            arrived(rs_r.at[s, j, rr], ra_s.at[s, j, d], ra_r.at[s, j, rr])
            total = total + rs_r[s, j, rr].astype(F32)
        wv[s, j, rows(r, b), :] = total.astype(BF)
        mine = wv.at[s, j, rows(r, b), :]
        for d in range(1, R):
            send(mine, mine, rb_s.at[s, j, d], rb_r.at[s, j, r], (rr_of(d), c))

    def p4_wait(s, j):
        for d in range(1, R):
            rr = rr_of(d)
            arrived(wv.at[s, j, rows(rr, b), :], rb_s.at[s, j, d], rb_r.at[s, j, rr])
        copy = pltpu.make_async_copy(
            wv.at[s, j], wh_out.at[s, :, pl.ds(j * n, n)], out_sem.at[s, j])
        copy.start()
        local.append(copy)

    def p4(s, j):
        if s == 0:
            ready("f0")

            def put(at, value):
                acc[j, at, :] = value

            matmul(f_v.at[0], wv.at[s, j], kb, put)
        else:
            ready("l")

            def put(at, value):
                acc[j, at, :] = acc2[j, at, :] + value

            matmul(l_v.at[0], wv.at[s, j], kb, put)
        for zz in range(Z):
            ps_s[s, j, zz] = acc[j, rows(zz * 2 + 1 - k, b), :].astype(BF)
        send(ps_s.at[s, j], ps_r.at[s, j], pa_s.at[s, j], pa_r.at[s, j], partner)

    def p5(s, j):
        arrived(ps_r.at[s, j], pa_s.at[s, j], pa_r.at[s, j])
        for d in range(1, Z):
            zz = zz_of(d)
            value = acc[j, rows(zz * 2 + k, b), :] + ps_r[s, j, zz].astype(F32)
            zs_s[s, j, zz] = value.astype(BF)
            send(zs_s.at[s, j, zz], zs_r.at[s, j, z],
                 za_s.at[s, j, d], za_r.at[s, j, z], zpeer(zz))
        if s == 0:
            ready("f1")

            def put(at, value):
                acc2[j, at, :] = value

            matmul(f_v.at[1], wv.at[0, j], kb, put)

    def p6(s, j):
        total = acc[j, rows(c, b), :] + ps_r[s, j, z].astype(F32)
        for d in range(1, Z):
            zz = zz_of(d)
            arrived(zs_r.at[s, j, zz], za_s.at[s, j, d], za_r.at[s, j, zz])
            total = total + zs_r[s, j, zz].astype(F32)
        value = m_v[s + 1, :, j * n:(j + 1) * n] - total
        if s == 0:
            xg[1, j, rows(c, b), :] = value.astype(BF)
            give_x(1, j)
        else:
            tr_v[:, j * n:(j + 1) * n] = value

    h = e // R // 2

    def gram(s):
        for j in range(CHUNKS):
            value = lax.dot_general(
                wv[s, 0], wv[s, j], (((0,), (0,)), ((), ())), preferred_element_type=F32)
            at = slice(j * n, (j + 1) * n)
            if s == 0:
                pacc[:, at] = value
            else:
                pacc[:, at] = pacc[:, at] + value

    def q0():
        gram(1)
        send(pacc.at[rows(r * 2 + 1 - k, h), :], pp_r, q_s.at[0], q_r.at[0], partner)

    def q1():
        arrived(pp_r, q_s.at[0], q_r.at[0])
        pz[z] = pacc[rows(r * 2 + k, h), :] + pp_r[...]
        for d in range(1, Z):
            send(pz.at[z], pz.at[z], qz_s.at[d], qz_r.at[z], zpeer(zz_of(d)))

    def q2():
        for d in range(1, Z):
            zz = zz_of(d)
            arrived(pz.at[zz], qz_s.at[d], qz_r.at[zz])
        total = pz[0]
        for zz in range(1, Z):
            total = total + pz[zz]
        pg[k, r] = total
        mine = pg.at[k, r]
        for d in range(1, R):
            send(mine, mine, qr_s.at[d], qr_r.at[r], (rr_of(d), c))

    def q3():
        for d in range(1, R):
            rr = rr_of(d)
            arrived(pg.at[k, rr], qr_s.at[d], qr_r.at[rr])
        send(pg.at[k], pg.at[k], q_s.at[1], q_r.at[1], partner)

    def q4():
        arrived(pg.at[1 - k], q_s.at[1], q_r.at[1])
        for kk in range(2):
            copy = pltpu.make_async_copy(pg.at[kk], pr_out.at[:, kk], po_sem.at[kk])
            copy.start()
            local.append(copy)

    def full4(s, j):
        p4_wait(s, j)
        p4(s, j)

    A, B = 0, 1
    ready("m")
    p0(A)
    p0(B)
    p1(0, A)
    p2(0, A)
    p3(0, A)
    p1(0, B)
    p2(0, B)
    full4(0, A)
    p5(0, A)
    p3(0, B)
    full4(0, B)
    p6(0, A)
    p5(0, B)
    gram(0)
    p1(1, A)
    p2(1, A)
    p3(1, A)
    p6(0, B)
    full4(1, A)
    p5(1, A)
    p1(1, B)
    p2(1, B)
    p3(1, B)
    p6(1, A)
    p4_wait(1, B)
    q0()
    p4(1, B)
    q1()
    p5(1, B)
    q2()
    q3()
    p6(1, B)
    copy = pltpu.make_async_copy(tr_v, tr_out.at[0], po_sem.at[2])
    copy.start()
    local.append(copy)
    q4()
    for copy in sends:
        copy.wait_send()
    for copy in local:
        copy.wait()


def body(R, Z, m, p, f, l):
    b, cols = m.shape[1], m.shape[2]
    n = cols // CHUNKS
    e = cols // 2
    rb, kb = R * b, 2 * Z * b
    h = e // R // 2
    sem = pltpu.SemaphoreType.DMA
    V = pltpu.VMEM
    flops = 2 * 5 * rb * kb * cols
    any_spec = pl.BlockSpec(memory_space=pl.ANY)
    whitened, trailing, proj = pl.pallas_call(
        functools.partial(kernel, R, Z, b, n, e),
        out_shape=(
            jax.ShapeDtypeStruct((2, rb, cols), BF),
            jax.ShapeDtypeStruct((1, b, cols), F32),
            jax.ShapeDtypeStruct((R, 2, h, cols), F32),
        ),
        in_specs=[any_spec] * 4,
        out_specs=(any_spec,) * 3,
        scratch_shapes=[
            V(m.shape, F32), V(p.shape, BF), V(f.shape, BF), V(l.shape, BF),
            V((2, CHUNKS, kb, n), BF),
            V((2, CHUNKS, rb, n), BF), V((2, CHUNKS, R, b, n), BF),
            V((2, CHUNKS, rb, n), BF),
            V((CHUNKS, kb, n), F32), V((CHUNKS, kb, n), F32),
            V((2, CHUNKS, Z, b, n), BF), V((2, CHUNKS, Z, b, n), BF),
            V((2, CHUNKS, Z, b, n), BF), V((2, CHUNKS, Z, b, n), BF),
            V((b, cols), F32),
            V((e, cols), F32), V((h, cols), F32), V((Z, h, cols), F32),
            V((2, R, h, cols), F32),
            sem((6,)), sem((2, CHUNKS)), sem((3,)),
            sem((2, CHUNKS, Z)), sem((2, CHUNKS, Z)),
            sem((2, CHUNKS, Z)), sem((2, CHUNKS, Z)),
            sem((2, CHUNKS, R)), sem((2, CHUNKS, R)),
            sem((2, CHUNKS, R)), sem((2, CHUNKS, R)),
            sem((2, CHUNKS)), sem((2, CHUNKS)),
            sem((2, CHUNKS, Z)), sem((2, CHUNKS, Z)),
            sem((2,)), sem((2,)), sem((Z,)), sem((Z,)), sem((R,)), sem((R,)),
        ],
        compiler_params=pltpu.CompilerParams(
            collective_id=0, has_side_effects=True, vmem_limit_bytes=60 * 2**20),
        cost_estimate=pl.CostEstimate(
            flops=flops, bytes_accessed=10 * rb * kb, transcendentals=0),
    )(m, p, f, l)
    return whitened, trailing, proj.reshape(e, cols)


def solution(mesh):
    R, Z = mesh.shape["row"], mesh.shape["col"] // 2
    in_specs = (
        P(None, ("row", "col"), None),
        P(None, "col", "row"),
        P(None, "row", "col"),
        P(None, "row", "col"),
    )
    out_specs = (P(None, "col", None), P(None, ("row", "col"), None), P())
    return jax.shard_map(
        functools.partial(body, R, Z), mesh=mesh, in_specs=in_specs, out_specs=out_specs,
        check_vma=False,
    )
```

```python
import functools

import jax
import jax.numpy as jnp
from jax import lax
from jax.experimental import pallas as pl
from jax.experimental.pallas import tpu as pltpu
from jax.sharding import PartitionSpec as P

MESH = pl.DeviceIdType.MESH
BF = jnp.bfloat16
F32 = jnp.float32
CHUNKS = 2


def kernel(
    R, Z, b, n, e,
    m_h, p_h, f_h, l_h,
    wh_out, tr_out, pr_out,
    m_v, p_v, f_v, l_v, xg, rs_s, rs_r, wv, acc, acc2, ps_s, ps_r, zs_s, zs_r, tr_v,
    pacc, pp_r, pz, pg, zi_r,
    ld_sem, out_sem, po_sem,
    xz_s, xz_r, xp_s, xp_r, ra_s, ra_r, rb_s, rb_r, pa_s, pa_r, za_s, za_r,
    q_s, q_r, qz_s, qz_r, qr_s, qr_r, io_s, io_r, t_s, t_r,
):
    r = lax.axis_index("row")
    c = lax.axis_index("col")
    z = lax.div(c, 2)
    k = lax.rem(c, 2)
    rb, kb = R * b, 2 * Z * b
    partner = (r, z * 2 + 1 - k)

    def zpeer(zz):
        return (r, zz * 2 + k)

    left = z < Z // 2
    edge = (z == 0) | (z == Z - 1)
    mid = (z == Z // 2 - 1) | (z == Z // 2)
    mid_slot = jnp.where(mid, 1, 0)
    inward = zpeer(jnp.where(left, z + 1, z - 1))
    outward = zpeer(jnp.where(left, jnp.maximum(z - 1, 0), jnp.minimum(z + 1, Z - 1)))

    def zz_of(d):
        return lax.rem(z + d, Z)

    def rr_of(d):
        return lax.rem(r + d, R)

    def rows(block, size, count=None):
        return pl.ds(pl.multiple_of(block * size, size), size if count is None else count)

    loads = {}

    def load(name, index, src, dst):
        copy = pltpu.make_async_copy(src, dst, ld_sem.at[index])
        copy.start()
        loads[name] = copy

    load("m", 0, m_h, m_v)
    load("p0", 1, p_h.at[0], p_v.at[0])
    load("f0", 2, f_h.at[0], f_v.at[0])
    load("p1", 3, p_h.at[1], p_v.at[1])
    load("f1", 4, f_h.at[1], f_v.at[1])
    load("l", 5, l_h.at[0], l_v.at[0])

    barrier = pltpu.get_barrier_semaphore()
    peers = [partner] + [zpeer(zz_of(d)) for d in range(1, Z)]
    peers += [(rr_of(d), c) for d in range(1, R)]
    for peer in peers:
        pl.semaphore_signal(barrier, inc=1, device_id=peer, device_id_type=MESH)
    pl.semaphore_wait(barrier, len(peers))

    sends = []
    local = []

    def send(src, dst, ssem, rsem, device, into=None):
        copy = pltpu.make_async_remote_copy(
            src_ref=src, dst_ref=dst, send_sem=ssem, recv_sem=rsem,
            device_id=device, device_id_type=MESH,
        )
        copy.start()
        if into is None:
            sends.append(copy)

    def arrived(dst, ssem, rsem):
        pltpu.make_async_remote_copy(
            src_ref=dst, dst_ref=dst, send_sem=ssem, recv_sem=rsem,
            device_id=partner, device_id_type=MESH,
        ).wait_recv()

    waited = set()

    def ready(name):
        if name not in waited:
            waited.add(name)
            loads[name].wait()

    def matmul(a, x, total, put):
        tile = min(512, total)

        def step(i, carry):
            at = pl.ds(pl.multiple_of(i * tile, tile), tile)
            put(at, jnp.dot(a[at, :], x[...], preferred_element_type=F32))
            return carry

        lax.fori_loop(0, total // tile, step, 0)

    def xblock(s, j, cc):
        return xg.at[s, j, rows(cc, b), :]

    def give_x(s, j):
        mine = xblock(s, j, c)
        for d in range(1, Z):
            send(mine, mine, xz_s.at[s, j, d], xz_r.at[s, j, z], zpeer(zz_of(d)))
        send(mine, mine, xp_s.at[s, j, z], xp_r.at[s, j, z], partner)

    def p0(j):
        xg[0, j, rows(c, b), :] = m_v[0, :, j * n:(j + 1) * n].astype(BF)
        give_x(0, j)

    def p1(s, j):
        for d in range(1, Z):
            zz = zz_of(d)
            blk = xblock(s, j, zz * 2 + k)
            arrived(blk, xz_s.at[s, j, d], xz_r.at[s, j, zz])
            send(blk, blk, xp_s.at[s, j, zz], xp_r.at[s, j, zz], partner)

    def p2(s, j):
        for d in range(Z):
            zz = zz_of(d)
            arrived(xblock(s, j, zz * 2 + 1 - k), xp_s.at[s, j, zz], xp_r.at[s, j, zz])
        ready("p%d" % s)

        def put(at, value):
            acc[j, at, :] = value
            rs_s[s, j, at, :] = value.astype(BF)

        matmul(p_v.at[s], xg.at[s, j], rb, put)
        for d in range(1, R):
            rr = rr_of(d)
            send(rs_s.at[s, j, rows(rr, b), :], rs_r.at[s, j, r],
                 ra_s.at[s, j, d], ra_r.at[s, j, r], (rr, c))

    def p3(s, j):
        total = acc[j, rows(r, b), :]
        for d in range(1, R):
            rr = rr_of(d)
            arrived(rs_r.at[s, j, rr], ra_s.at[s, j, d], ra_r.at[s, j, rr])
            total = total + rs_r[s, j, rr].astype(F32)
        wv[s, j, rows(r, b), :] = total.astype(BF)
        mine = wv.at[s, j, rows(r, b), :]
        for d in range(1, R):
            send(mine, mine, rb_s.at[s, j, d], rb_r.at[s, j, r], (rr_of(d), c))

    def p4_wait(s, j):
        for d in range(1, R):
            rr = rr_of(d)
            arrived(wv.at[s, j, rows(rr, b), :], rb_s.at[s, j, d], rb_r.at[s, j, rr])
        copy = pltpu.make_async_copy(
            wv.at[s, j], wh_out.at[s, :, pl.ds(j * n, n)], out_sem.at[s, j])
        copy.start()
        local.append(copy)

    def p4(s, j):
        if s == 0:
            ready("f0")

            def put(at, value):
                acc[j, at, :] = value

            matmul(f_v.at[0], wv.at[s, j], kb, put)
        else:
            ready("l")

            def put(at, value):
                acc[j, at, :] = acc2[j, at, :] + value

            matmul(l_v.at[0], wv.at[s, j], kb, put)
        for zz in range(Z):
            ps_s[s, j, zz] = acc[j, rows(zz * 2 + 1 - k, b), :].astype(BF)
        send(ps_s.at[s, j], ps_r.at[s, j], pa_s.at[s, j], pa_r.at[s, j], partner)

    def f1(j):
        ready("f1")

        def put(at, value):
            acc2[j, at, :] = value

        matmul(f_v.at[1], wv.at[0, j], kb, put)

    def pair(s, j):
        arrived(ps_r.at[s, j], pa_s.at[s, j], pa_r.at[s, j])

    def s1(j, q):
        at = rows(q * 2 + k, b)
        own = jnp.where(z == q, m_v[1, :, j * n:(j + 1) * n], 0.0)
        acc[j, at, :] = acc[j, at, :] + ps_r[0, j, q].astype(F32) - own

        @pl.when(jnp.logical_not(edge))
        def _():
            arrived(zi_r.at[0, j, q], io_s.at[j, q], io_r.at[0, j, q])
            acc[j, at, :] = acc[j, at, :] + zi_r[0, j, q].astype(F32)

        zs_s[0, j, q] = acc[j, at, :].astype(BF)
        send(zs_s.at[0, j, q], zi_r.at[mid_slot, j, q],
             io_s.at[j, q], io_r.at[mid_slot, j, q], inward)

    def s2(j, q):
        at = rows(q * 2 + k, b)
        blk = xg.at[1, j, at, :]

        @pl.when(mid)
        def _():
            arrived(zi_r.at[1, j, q], io_s.at[j, q], io_r.at[1, j, q])
            xg[1, j, at, :] = (-(acc[j, at, :] + zi_r[1, j, q].astype(F32))).astype(BF)

        @pl.when(jnp.logical_not(mid))
        def _():
            arrived(blk, t_s.at[j, q], t_r.at[j, q])

        @pl.when(jnp.logical_not(edge))
        def _():
            send(blk, blk, t_s.at[j, q], t_r.at[j, q], outward, False)

        send(blk, blk, xp_s.at[1, j, q], xp_r.at[1, j, q], partner)

    def p5(j):
        pair(1, j)
        for d in range(1, Z):
            zz = zz_of(d)
            value = acc[j, rows(zz * 2 + k, b), :] + ps_r[1, j, zz].astype(F32)
            zs_s[1, j, zz] = value.astype(BF)
            send(zs_s.at[1, j, zz], zs_r.at[j, z],
                 za_s.at[j, d], za_r.at[j, z], zpeer(zz))

    def p6(j):
        total = acc[j, rows(c, b), :] + ps_r[1, j, z].astype(F32)
        for d in range(1, Z):
            zz = zz_of(d)
            arrived(zs_r.at[j, zz], za_s.at[j, d], za_r.at[j, zz])
            total = total + zs_r[j, zz].astype(F32)
        tr_v[:, j * n:(j + 1) * n] = m_v[2, :, j * n:(j + 1) * n] - total

    h = e // R // 2

    def gram(s):
        for j in range(CHUNKS):
            value = lax.dot_general(
                wv[s, 0], wv[s, j], (((0,), (0,)), ((), ())), preferred_element_type=F32)
            at = slice(j * n, (j + 1) * n)
            if s == 0:
                pacc[:, at] = value
            else:
                pacc[:, at] = pacc[:, at] + value

    def q0():
        gram(1)
        send(pacc.at[rows(r * 2 + 1 - k, h), :], pp_r, q_s.at[0], q_r.at[0], partner)

    def q1():
        arrived(pp_r, q_s.at[0], q_r.at[0])
        pz[z] = pacc[rows(r * 2 + k, h), :] + pp_r[...]
        for d in range(1, Z):
            send(pz.at[z], pz.at[z], qz_s.at[d], qz_r.at[z], zpeer(zz_of(d)))

    def q2():
        for d in range(1, Z):
            zz = zz_of(d)
            arrived(pz.at[zz], qz_s.at[d], qz_r.at[zz])
        total = pz[0]
        for zz in range(1, Z):
            total = total + pz[zz]
        pg[k, r] = total
        mine = pg.at[k, r]
        for d in range(1, R):
            send(mine, mine, qr_s.at[d], qr_r.at[r], (rr_of(d), c))

    def q3():
        for d in range(1, R):
            rr = rr_of(d)
            arrived(pg.at[k, rr], qr_s.at[d], qr_r.at[rr])
        send(pg.at[k], pg.at[k], q_s.at[1], q_r.at[1], partner)

    def q4():
        arrived(pg.at[1 - k], q_s.at[1], q_r.at[1])
        for kk in range(2):
            copy = pltpu.make_async_copy(pg.at[kk], pr_out.at[:, kk], po_sem.at[kk])
            copy.start()
            local.append(copy)

    def full4(s, j):
        p4_wait(s, j)
        p4(s, j)

    A, B = 0, 1
    ready("m")
    half = (Z + 1) // 2
    p0(A)
    p1(0, A)
    p0(B)
    p2(0, A)
    p3(0, A)
    p1(0, B)
    p2(0, B)
    full4(0, A)
    pair(0, A)
    s1(A, 0)
    f1(A)
    p3(0, B)
    for q in range(1, Z - 1):
        s1(A, q)
    full4(0, B)
    s1(A, Z - 1)
    for q in range(half):
        s2(A, q)
    pair(0, B)
    s1(B, 0)
    for q in range(half, Z):
        s2(A, q)
    s1(B, 1)
    p2(1, A)
    for q in range(2, Z):
        s1(B, q)
    s2(B, 0)
    p3(1, A)
    for q in range(1, Z):
        s2(B, q)
    f1(B)
    full4(1, A)
    p2(1, B)
    p5(A)
    gram(0)
    p3(1, B)
    p4_wait(1, B)
    q0()
    p4(1, B)
    q1()
    p6(A)
    p5(B)
    q2()
    q3()
    p6(B)
    copy = pltpu.make_async_copy(tr_v, tr_out.at[0], po_sem.at[2])
    copy.start()
    local.append(copy)
    q4()
    for copy in sends:
        copy.wait_send()

    @pl.when(jnp.logical_not(edge))
    def _():
        for j in range(CHUNKS):
            for q in range(Z):
                blk = xg.at[1, j, rows(q * 2 + k, b), :]
                pltpu.make_async_remote_copy(
                    src_ref=blk, dst_ref=blk, send_sem=t_s.at[j, q], recv_sem=t_r.at[j, q],
                    device_id=outward, device_id_type=MESH,
                ).wait_send()

    for copy in local:
        copy.wait()


def body(R, Z, m, p, f, l):
    b, cols = m.shape[1], m.shape[2]
    n = cols // CHUNKS
    e = cols // 2
    rb, kb = R * b, 2 * Z * b
    h = e // R // 2
    sem = pltpu.SemaphoreType.DMA
    V = pltpu.VMEM
    flops = 2 * 5 * rb * kb * cols
    any_spec = pl.BlockSpec(memory_space=pl.ANY)
    whitened, trailing, proj = pl.pallas_call(
        functools.partial(kernel, R, Z, b, n, e),
        out_shape=(
            jax.ShapeDtypeStruct((2, rb, cols), BF),
            jax.ShapeDtypeStruct((1, b, cols), F32),
            jax.ShapeDtypeStruct((R, 2, h, cols), F32),
        ),
        in_specs=[any_spec] * 4,
        out_specs=(any_spec,) * 3,
        scratch_shapes=[
            V(m.shape, F32), V(p.shape, BF), V(f.shape, BF), V(l.shape, BF),
            V((2, CHUNKS, kb, n), BF),
            V((2, CHUNKS, rb, n), BF), V((2, CHUNKS, R, b, n), BF),
            V((2, CHUNKS, rb, n), BF),
            V((CHUNKS, kb, n), F32), V((CHUNKS, kb, n), F32),
            V((2, CHUNKS, Z, b, n), BF), V((2, CHUNKS, Z, b, n), BF),
            V((2, CHUNKS, Z, b, n), BF), V((CHUNKS, Z, b, n), BF),
            V((b, cols), F32),
            V((e, cols), F32), V((h, cols), F32), V((Z, h, cols), F32),
            V((2, R, h, cols), F32), V((2, CHUNKS, Z, b, n), BF),
            sem((6,)), sem((2, CHUNKS)), sem((3,)),
            sem((2, CHUNKS, Z)), sem((2, CHUNKS, Z)),
            sem((2, CHUNKS, Z)), sem((2, CHUNKS, Z)),
            sem((2, CHUNKS, R)), sem((2, CHUNKS, R)),
            sem((2, CHUNKS, R)), sem((2, CHUNKS, R)),
            sem((2, CHUNKS)), sem((2, CHUNKS)),
            sem((CHUNKS, Z)), sem((CHUNKS, Z)),
            sem((2,)), sem((2,)), sem((Z,)), sem((Z,)), sem((R,)), sem((R,)),
            sem((CHUNKS, Z)), sem((2, CHUNKS, Z)), sem((CHUNKS, Z)), sem((CHUNKS, Z)),
        ],
        compiler_params=pltpu.CompilerParams(
            collective_id=0, has_side_effects=True, vmem_limit_bytes=60 * 2**20),
        cost_estimate=pl.CostEstimate(
            flops=flops, bytes_accessed=10 * rb * kb, transcendentals=0),
    )(m, p, f, l)
    return whitened, trailing, proj.reshape(e, cols)


def solution(mesh):
    R, Z = mesh.shape["row"], mesh.shape["col"] // 2
    in_specs = (
        P(None, ("row", "col"), None),
        P(None, "col", "row"),
        P(None, "row", "col"),
        P(None, "row", "col"),
    )
    out_specs = (P(None, "col", None), P(None, ("row", "col"), None), P())
    return jax.shard_map(
        functools.partial(body, R, Z), mesh=mesh, in_specs=in_specs, out_specs=out_specs,
        check_vma=False,
    )
```

```python
import functools

import jax
import jax.numpy as jnp
from jax import lax
from jax.experimental import pallas as pl
from jax.experimental.pallas import tpu as pltpu
from jax.sharding import PartitionSpec as P

MESH = pl.DeviceIdType.MESH
BF = jnp.bfloat16
F32 = jnp.float32
CHUNKS = 2


def kernel(
    R, Z, b, n, e,
    m_h, p_h, f_h, l_h,
    wh_out, tr_out, pr_out,
    m_v, p_v, f_v, l_v, xg, rs_s, rs_r, wv, acc, acc2, ps_s, ps_r, zs_s, zs_r, tr_v,
    pacc, pp_r, pz, pg, zi_r, accp,
    ld_sem, out_sem, po_sem,
    xz_s, xz_r, xp_s, xp_r, ra_s, ra_r, rb_s, rb_r, pa_s, pa_r, za_s, za_r,
    q_s, q_r, qz_s, qz_r, qr_s, qr_r, io_s, io_r, t_s, t_r,
):
    r = lax.axis_index("row")
    c = lax.axis_index("col")
    z = lax.div(c, 2)
    k = lax.rem(c, 2)
    rb, kb = R * b, 2 * Z * b
    partner = (r, z * 2 + 1 - k)

    def zpeer(zz):
        return (r, zz * 2 + k)

    left = z < Z // 2
    edge = (z == 0) | (z == Z - 1)
    mid = (z == Z // 2 - 1) | (z == Z // 2)
    mid_slot = jnp.where(mid, 1, 0)
    inward = zpeer(jnp.where(left, z + 1, z - 1))
    outward = zpeer(jnp.where(left, jnp.maximum(z - 1, 0), jnp.minimum(z + 1, Z - 1)))

    def zz_of(d):
        return lax.rem(z + d, Z)

    def rr_of(d):
        return lax.rem(r + d, R)

    def rows(block, size, count=None):
        return pl.ds(pl.multiple_of(block * size, size), size if count is None else count)

    loads = {}

    def load(name, index, src, dst):
        copy = pltpu.make_async_copy(src, dst, ld_sem.at[index])
        copy.start()
        loads[name] = copy

    load("m", 0, m_h, m_v)
    load("p0", 1, p_h.at[0], p_v.at[0])
    load("f0", 2, f_h.at[0], f_v.at[0])
    load("p1", 3, p_h.at[1], p_v.at[1])
    load("f1", 4, f_h.at[1], f_v.at[1])
    load("l", 5, l_h.at[0], l_v.at[0])

    barrier = pltpu.get_barrier_semaphore()
    peers = [partner] + [zpeer(zz_of(d)) for d in range(1, Z)]
    peers += [(rr_of(d), c) for d in range(1, R)]
    for peer in peers:
        pl.semaphore_signal(barrier, inc=1, device_id=peer, device_id_type=MESH)
    pl.semaphore_wait(barrier, len(peers))

    sends = []
    local = []

    def send(src, dst, ssem, rsem, device, into=None):
        copy = pltpu.make_async_remote_copy(
            src_ref=src, dst_ref=dst, send_sem=ssem, recv_sem=rsem,
            device_id=device, device_id_type=MESH,
        )
        copy.start()
        if into is None:
            sends.append(copy)

    def arrived(dst, ssem, rsem):
        pltpu.make_async_remote_copy(
            src_ref=dst, dst_ref=dst, send_sem=ssem, recv_sem=rsem,
            device_id=partner, device_id_type=MESH,
        ).wait_recv()

    waited = set()

    def ready(name):
        if name not in waited:
            waited.add(name)
            loads[name].wait()

    def matmul(a, x, total, put):
        tile = min(512, total)

        def step(i, carry):
            at = pl.ds(pl.multiple_of(i * tile, tile), tile)
            put(at, jnp.dot(a[at, :], x[...], preferred_element_type=F32))
            return carry

        lax.fori_loop(0, total // tile, step, 0)

    def xblock(s, j, cc):
        return xg.at[s, j, rows(cc, b), :]

    def give_x(s, j):
        mine = xblock(s, j, c)
        for d in range(1, Z):
            send(mine, mine, xz_s.at[s, j, d], xz_r.at[s, j, z], zpeer(zz_of(d)))
        send(mine, mine, xp_s.at[s, j, z], xp_r.at[s, j, z], partner)

    def p0(j):
        xg[0, j, rows(c, b), :] = m_v[0, :, j * n:(j + 1) * n].astype(BF)
        give_x(0, j)

    def from_z(s, j, d):
        zz = zz_of(d)
        blk = xblock(s, j, zz * 2 + k)
        arrived(blk, xz_s.at[s, j, d], xz_r.at[s, j, zz])
        send(blk, blk, xp_s.at[s, j, zz], xp_r.at[s, j, zz], partner)

    split = (2 * b) % 128 == 0

    def columns(zz):
        return pl.ds(pl.multiple_of(zz * 2 * b, 2 * b), 2 * b) if split else slice(None)

    def taken(s, j, zz):
        return xg.at[s, j, rows(zz, 2 * b), :] if split else xg.at[s, j]

    def kblock(s, j, zz, first):
        arrived(xblock(s, j, zz * 2 + 1 - k), xp_s.at[s, j, zz], xp_r.at[s, j, zz])
        ready("p%d" % s)
        if split:
            def put(at, value):
                accp[j, at, :] = value if first else accp[j, at, :] + value

            matmul(p_v.at[s, :, columns(zz)], taken(s, j, zz), rb, put)

    def klast(s, j, zz):
        arrived(xblock(s, j, zz * 2 + 1 - k), xp_s.at[s, j, zz], xp_r.at[s, j, zz])
        ready("p%d" % s)
        for d in list(range(1, R)) + [0]:
            rr = rr_of(d)
            at = rows(rr, b)
            value = jnp.dot(p_v[s, at, columns(zz)], taken(s, j, zz)[...],
                            preferred_element_type=F32)
            if split and Z > 1:
                value = accp[j, at, :] + value
            if d:
                rs_s[s, j, at, :] = value.astype(BF)
                send(rs_s.at[s, j, at, :], rs_r.at[s, j, r],
                     ra_s.at[s, j, d], ra_r.at[s, j, r], (rr, c))
            else:
                accp[j, at, :] = value

    def gather(j):
        for d in range(1, Z):
            from_z(0, j, d)
            kblock(0, j, zz_of(d - 1), d == 1)

    def first_product(j):
        klast(0, j, zz_of(Z - 1))

    def p3(s, j):
        total = accp[j, rows(r, b), :]
        for d in range(1, R):
            rr = rr_of(d)
            arrived(rs_r.at[s, j, rr], ra_s.at[s, j, d], ra_r.at[s, j, rr])
            total = total + rs_r[s, j, rr].astype(F32)
        wv[s, j, rows(r, b), :] = total.astype(BF)
        mine = wv.at[s, j, rows(r, b), :]
        for d in range(1, R):
            send(mine, mine, rb_s.at[s, j, d], rb_r.at[s, j, r], (rr_of(d), c))

    def p4_wait(s, j):
        for d in range(1, R):
            rr = rr_of(d)
            arrived(wv.at[s, j, rows(rr, b), :], rb_s.at[s, j, d], rb_r.at[s, j, rr])
        copy = pltpu.make_async_copy(
            wv.at[s, j], wh_out.at[s, :, pl.ds(j * n, n)], out_sem.at[s, j])
        copy.start()
        local.append(copy)

    def tile(s, j, block):
        at = rows(block, b)
        if s == 0:
            return jnp.dot(f_v[0, at, :], wv[0, j], preferred_element_type=F32)
        return acc2[j, at, :] + jnp.dot(l_v[0, at, :], wv[1, j], preferred_element_type=F32)

    def p4(s, j):
        ready("l" if s else "f0")
        for i in range(Z):
            q = zz_of(1 + i) if s else i
            ps_s[s, j, q] = tile(s, j, q * 2 + 1 - k).astype(BF)
            send(ps_s.at[s, j, q], ps_r.at[s, j, q], pa_s.at[s, j, q], pa_r.at[s, j, q], partner)

    def paired(s, j, q):
        value = tile(s, j, q * 2 + k)
        arrived(ps_r.at[s, j, q], pa_s.at[s, j, q], pa_r.at[s, j, q])
        return value + ps_r[s, j, q].astype(F32)

    def f1(j):
        ready("f1")

        def put(at, value):
            acc2[j, at, :] = value

        matmul(f_v.at[1], wv.at[0, j], kb, put)

    def s1(j, q):
        at = rows(q * 2 + k, b)
        own = jnp.where(z == q, m_v[1, :, j * n:(j + 1) * n], 0.0)
        acc[j, at, :] = paired(0, j, q) - own

        @pl.when(jnp.logical_not(edge))
        def _():
            arrived(zi_r.at[0, j, q], io_s.at[j, q], io_r.at[0, j, q])
            acc[j, at, :] = acc[j, at, :] + zi_r[0, j, q].astype(F32)

        zs_s[0, j, q] = acc[j, at, :].astype(BF)
        send(zs_s.at[0, j, q], zi_r.at[mid_slot, j, q],
             io_s.at[j, q], io_r.at[mid_slot, j, q], inward)

    def s2(j, q):
        at = rows(q * 2 + k, b)
        blk = xg.at[1, j, at, :]

        @pl.when(mid)
        def _():
            arrived(zi_r.at[1, j, q], io_s.at[j, q], io_r.at[1, j, q])
            xg[1, j, at, :] = (-(acc[j, at, :] + zi_r[1, j, q].astype(F32))).astype(BF)

        @pl.when(jnp.logical_not(mid))
        def _():
            arrived(blk, t_s.at[j, q], t_r.at[j, q])

        @pl.when(jnp.logical_not(edge))
        def _():
            send(blk, blk, t_s.at[j, q], t_r.at[j, q], outward, False)

        send(blk, blk, xp_s.at[1, j, q], xp_r.at[1, j, q], partner)

    def p5(j):
        for d in range(1, Z):
            zz = zz_of(d)
            zs_s[1, j, zz] = paired(1, j, zz).astype(BF)
            send(zs_s.at[1, j, zz], zs_r.at[j, z],
                 za_s.at[j, d], za_r.at[j, z], zpeer(zz))
        acc[j, rows(c, b), :] = paired(1, j, z)

    def p6(j):
        total = acc[j, rows(c, b), :]
        for d in range(1, Z):
            zz = zz_of(d)
            arrived(zs_r.at[j, zz], za_s.at[j, d], za_r.at[j, zz])
            total = total + zs_r[j, zz].astype(F32)
        tr_v[:, j * n:(j + 1) * n] = m_v[2, :, j * n:(j + 1) * n] - total

    h = e // R // 2

    def gram(s):
        for j in range(CHUNKS):
            value = lax.dot_general(
                wv[s, 0], wv[s, j], (((0,), (0,)), ((), ())), preferred_element_type=F32)
            at = slice(j * n, (j + 1) * n)
            if s == 0:
                pacc[:, at] = value
            else:
                pacc[:, at] = pacc[:, at] + value

    def q0():
        gram(1)
        send(pacc.at[rows(r * 2 + 1 - k, h), :], pp_r, q_s.at[0], q_r.at[0], partner)

    def q1():
        arrived(pp_r, q_s.at[0], q_r.at[0])
        pz[z] = pacc[rows(r * 2 + k, h), :] + pp_r[...]
        for d in range(1, Z):
            send(pz.at[z], pz.at[z], qz_s.at[d], qz_r.at[z], zpeer(zz_of(d)))

    def q2():
        for d in range(1, Z):
            zz = zz_of(d)
            arrived(pz.at[zz], qz_s.at[d], qz_r.at[zz])
        total = pz[0]
        for zz in range(1, Z):
            total = total + pz[zz]
        pg[k, r] = total
        mine = pg.at[k, r]
        for d in range(1, R):
            send(mine, mine, qr_s.at[d], qr_r.at[r], (rr_of(d), c))

    def q3():
        for d in range(1, R):
            rr = rr_of(d)
            arrived(pg.at[k, rr], qr_s.at[d], qr_r.at[rr])
        send(pg.at[k], pg.at[k], q_s.at[1], q_r.at[1], partner)

    def q4():
        arrived(pg.at[1 - k], q_s.at[1], q_r.at[1])
        for kk in range(2):
            copy = pltpu.make_async_copy(pg.at[kk], pr_out.at[:, kk], po_sem.at[kk])
            copy.start()
            local.append(copy)

    def full4(s, j):
        p4_wait(s, j)
        p4(s, j)

    A, B = 0, 1
    ready("m")
    half = (Z + 1) // 2

    def back(j, q):
        s2(j, q)
        if q:
            kblock(1, j, q - 1, q == 1)

    p0(A)
    gather(A)
    p0(B)
    first_product(A)
    p3(0, A)
    gather(B)
    first_product(B)
    full4(0, A)
    s1(A, 0)
    p3(0, B)
    for q in range(1, Z - 1):
        s1(A, q)
    full4(0, B)
    s1(A, Z - 1)
    for q in range(half):
        back(A, q)
    s1(B, 0)
    for q in range(half, Z):
        back(A, q)
    s1(B, 1)
    klast(1, A, Z - 1)
    for q in range(2, Z):
        s1(B, q)
    f1(A)
    back(B, 0)
    p3(1, A)
    for q in range(1, Z):
        back(B, q)
    p4_wait(1, A)
    p4(1, A)
    klast(1, B, Z - 1)
    p5(A)
    f1(B)
    p3(1, B)
    gram(0)
    p4_wait(1, B)
    p4(1, B)
    q0()
    p5(B)
    q1()
    p6(A)
    q2()
    q3()
    p6(B)
    copy = pltpu.make_async_copy(tr_v, tr_out.at[0], po_sem.at[2])
    copy.start()
    local.append(copy)
    q4()
    for copy in sends:
        copy.wait_send()

    @pl.when(jnp.logical_not(edge))
    def _():
        for j in range(CHUNKS):
            for q in range(Z):
                blk = xg.at[1, j, rows(q * 2 + k, b), :]
                pltpu.make_async_remote_copy(
                    src_ref=blk, dst_ref=blk, send_sem=t_s.at[j, q], recv_sem=t_r.at[j, q],
                    device_id=outward, device_id_type=MESH,
                ).wait_send()

    for copy in local:
        copy.wait()


def hand_over(*refs):
    count = len(refs) // 2
    sems = refs[-1]
    copies = [
        pltpu.make_async_copy(refs[i], refs[count + i], sems.at[i]) for i in range(count)
    ]
    for copy in copies:
        copy.start()
    for copy in copies:
        copy.wait()


def body(R, Z, m, p, f, l):
    b, cols = m.shape[1], m.shape[2]
    n = cols // CHUNKS
    e = cols // 2
    rb, kb = R * b, 2 * Z * b
    h = e // R // 2
    sem = pltpu.SemaphoreType.DMA
    V = pltpu.VMEM
    flops = 2 * 5 * rb * kb * cols
    any_spec = pl.BlockSpec(memory_space=pl.ANY)
    whitened, trailing, proj = pl.pallas_call(
        functools.partial(kernel, R, Z, b, n, e),
        out_shape=(
            jax.ShapeDtypeStruct((2, rb, cols), BF),
            jax.ShapeDtypeStruct((1, b, cols), F32),
            jax.ShapeDtypeStruct((R, 2, h, cols), F32),
        ),
        in_specs=[any_spec] * 4,
        out_specs=(any_spec,) * 3,
        scratch_shapes=[
            V(m.shape, F32), V(p.shape, BF), V(f.shape, BF), V(l.shape, BF),
            V((2, CHUNKS, kb, n), BF),
            V((2, CHUNKS, rb, n), BF), V((2, CHUNKS, R, b, n), BF),
            V((2, CHUNKS, rb, n), BF),
            V((CHUNKS, kb, n), F32), V((CHUNKS, kb, n), F32),
            V((2, CHUNKS, Z, b, n), BF), V((2, CHUNKS, Z, b, n), BF),
            V((2, CHUNKS, Z, b, n), BF), V((CHUNKS, Z, b, n), BF),
            V((b, cols), F32),
            V((e, cols), F32), V((h, cols), F32), V((Z, h, cols), F32),
            V((2, R, h, cols), F32), V((2, CHUNKS, Z, b, n), BF), V((CHUNKS, rb, n), F32),
            sem((6,)), sem((2, CHUNKS)), sem((3,)),
            sem((2, CHUNKS, Z)), sem((2, CHUNKS, Z)),
            sem((2, CHUNKS, Z)), sem((2, CHUNKS, Z)),
            sem((2, CHUNKS, R)), sem((2, CHUNKS, R)),
            sem((2, CHUNKS, R)), sem((2, CHUNKS, R)),
            sem((2, CHUNKS, Z)), sem((2, CHUNKS, Z)),
            sem((CHUNKS, Z)), sem((CHUNKS, Z)),
            sem((2,)), sem((2,)), sem((Z,)), sem((Z,)), sem((R,)), sem((R,)),
            sem((CHUNKS, Z)), sem((2, CHUNKS, Z)), sem((CHUNKS, Z)), sem((CHUNKS, Z)),
        ],
        compiler_params=pltpu.CompilerParams(
            collective_id=0, has_side_effects=True, vmem_limit_bytes=60 * 2**20),
        cost_estimate=pl.CostEstimate(
            flops=flops, bytes_accessed=10 * rb * kb, transcendentals=0),
    )(m, p, f, l)
    results = (whitened, trailing, proj.reshape(e, cols))
    return pl.pallas_call(
        hand_over,
        out_shape=tuple(jax.ShapeDtypeStruct(a.shape, a.dtype) for a in results),
        in_specs=[any_spec] * 3,
        out_specs=(any_spec,) * 3,
        scratch_shapes=[sem((3,))],
    )(*results)


def solution(mesh):
    R, Z = mesh.shape["row"], mesh.shape["col"] // 2
    in_specs = (
        P(None, ("row", "col"), None),
        P(None, "col", "row"),
        P(None, "row", "col"),
        P(None, "row", "col"),
    )
    out_specs = (P(None, "col", None), P(None, ("row", "col"), None), P())
    return jax.shard_map(
        functools.partial(body, R, Z), mesh=mesh, in_specs=in_specs, out_specs=out_specs,
        check_vma=False,
    )
```

```python
import functools

import jax
import jax.numpy as jnp
from jax import lax
from jax.experimental import pallas as pl
from jax.experimental.pallas import tpu as pltpu
from jax.sharding import PartitionSpec as P

MESH = pl.DeviceIdType.MESH
BF = jnp.bfloat16
F32 = jnp.float32
CHUNKS = 2


def kernel(
    R, Z, b, n, e,
    m_h, p_h, f_h, l_h,
    wh_out, tr_out, pr_out,
    m_v, p_v, f_v, l_v, xg, rs_s, rs_r, wv, acc, acc2, ps_s, ps_r, zs_s, zs_r, tr_v,
    pacc, pp_r, pz, pg, zi_r,
    ld_sem, out_sem, po_sem,
    xz_s, xz_r, xp_s, xp_r, ra_s, ra_r, rb_s, rb_r, pa_s, pa_r, za_s, za_r,
    q_s, q_r, qz_s, qz_r, qr_s, qr_r, io_s, io_r, t_s, t_r,
):
    r = lax.axis_index("row")
    c = lax.axis_index("col")
    z = lax.div(c, 2)
    k = lax.rem(c, 2)
    rb, kb = R * b, 2 * Z * b
    partner = (r, z * 2 + 1 - k)

    def zpeer(zz):
        return (r, zz * 2 + k)

    left = z < Z // 2
    edge = (z == 0) | (z == Z - 1)
    mid = (z == Z // 2 - 1) | (z == Z // 2)
    mid_slot = jnp.where(mid, 1, 0)
    inward = zpeer(jnp.where(left, z + 1, z - 1))
    outward = zpeer(jnp.where(left, jnp.maximum(z - 1, 0), jnp.minimum(z + 1, Z - 1)))

    def zz_of(d):
        return lax.rem(z + d, Z)

    def rr_of(d):
        return lax.rem(r + d, R)

    def rows(block, size, count=None):
        return pl.ds(pl.multiple_of(block * size, size), size if count is None else count)

    loads = {}

    def load(name, index, src, dst):
        copy = pltpu.make_async_copy(src, dst, ld_sem.at[index])
        copy.start()
        loads[name] = copy

    load("m", 0, m_h, m_v)
    load("p0", 1, p_h.at[0], p_v.at[0])
    load("f0", 2, f_h.at[0], f_v.at[0])
    load("p1", 3, p_h.at[1], p_v.at[1])
    load("f1", 4, f_h.at[1], f_v.at[1])
    load("l", 5, l_h.at[0], l_v.at[0])

    barrier = pltpu.get_barrier_semaphore()
    peers = [partner] + [zpeer(zz_of(d)) for d in range(1, Z)]
    peers += [(rr_of(d), c) for d in range(1, R)]
    for peer in peers:
        pl.semaphore_signal(barrier, inc=1, device_id=peer, device_id_type=MESH)
    pl.semaphore_wait(barrier, len(peers))

    sends = []
    local = []

    def send(src, dst, ssem, rsem, device, into=None):
        copy = pltpu.make_async_remote_copy(
            src_ref=src, dst_ref=dst, send_sem=ssem, recv_sem=rsem,
            device_id=device, device_id_type=MESH,
        )
        copy.start()
        if into is None:
            sends.append(copy)

    def arrived(dst, ssem, rsem):
        pltpu.make_async_remote_copy(
            src_ref=dst, dst_ref=dst, send_sem=ssem, recv_sem=rsem,
            device_id=partner, device_id_type=MESH,
        ).wait_recv()

    waited = set()

    def ready(name):
        if name not in waited:
            waited.add(name)
            loads[name].wait()

    def matmul(a, x, dst, total, depth, init=True):
        tile = min(512, total)
        block = min(256, depth)

        def one(i, carry):
            at = pl.ds(pl.multiple_of(i * tile, tile), tile)

            def first(q, carry):
                dst[pl.ds(pl.multiple_of(i * tile + q * 16, 16), 16), :] = jnp.zeros((16, n), F32)
                return carry

            if init:
                lax.fori_loop(0, tile // 16, first, 0)

            def step(q, carry):
                deep = pl.ds(pl.multiple_of(q * block, block), block)
                dst[at, :] += jnp.dot(a[at, deep], x[deep, :], preferred_element_type=F32)
                return carry

            return lax.fori_loop(0, depth // block, step, carry)

        lax.fori_loop(0, total // tile, one, 0)

    def pieces(count, fn):
        size = min(32, b)

        def step(i, carry):
            def at(start=0):
                return pl.ds(pl.multiple_of(start + i * size, 16), size)

            fn(at)
            return carry

        lax.fori_loop(0, count // size, step, 0)

    def xblock(s, j, cc):
        return xg.at[s, j, rows(cc, b), :]

    def give_x(s, j):
        mine = xblock(s, j, c)
        for d in range(1, Z):
            send(mine, mine, xz_s.at[s, j, d], xz_r.at[s, j, z], zpeer(zz_of(d)))
        send(mine, mine, xp_s.at[s, j, z], xp_r.at[s, j, z], partner)

    def p0(j):
        def fn(at):
            xg[0, j, at(c * b), :] = m_v[0, at(), j * n:(j + 1) * n].astype(BF)

        pieces(b, fn)
        give_x(0, j)

    def p1(s, j):
        for d in range(1, Z):
            zz = zz_of(d)
            blk = xblock(s, j, zz * 2 + k)
            arrived(blk, xz_s.at[s, j, d], xz_r.at[s, j, zz])
            send(blk, blk, xp_s.at[s, j, zz], xp_r.at[s, j, zz], partner)

    def p2(s, j):
        for d in range(Z):
            zz = zz_of(d)
            arrived(xblock(s, j, zz * 2 + 1 - k), xp_s.at[s, j, zz], xp_r.at[s, j, zz])
        ready("p%d" % s)

        matmul(p_v.at[s], xg.at[s, j], acc.at[j], rb, kb)

        def fn(at):
            rs_s[s, j, at(), :] = acc[j, at(), :].astype(BF)

        pieces(rb, fn)
        for d in range(1, R):
            rr = rr_of(d)
            send(rs_s.at[s, j, rows(rr, b), :], rs_r.at[s, j, r],
                 ra_s.at[s, j, d], ra_r.at[s, j, r], (rr, c))

    def p3(s, j):
        for d in range(1, R):
            rr = rr_of(d)
            arrived(rs_r.at[s, j, rr], ra_s.at[s, j, d], ra_r.at[s, j, rr])

        def fn(at):
            total = acc[j, at(r * b), :]
            for d in range(1, R):
                total = total + rs_r[s, j, rr_of(d), at(), :].astype(F32)
            wv[s, j, at(r * b), :] = total.astype(BF)

        pieces(b, fn)
        mine = wv.at[s, j, rows(r, b), :]
        for d in range(1, R):
            send(mine, mine, rb_s.at[s, j, d], rb_r.at[s, j, r], (rr_of(d), c))

    def p4_wait(s, j):
        for d in range(1, R):
            rr = rr_of(d)
            arrived(wv.at[s, j, rows(rr, b), :], rb_s.at[s, j, d], rb_r.at[s, j, rr])
        copy = pltpu.make_async_copy(
            wv.at[s, j], wh_out.at[s, :, pl.ds(j * n, n)], out_sem.at[s, j])
        copy.start()
        local.append(copy)

    def p4(s, j):
        ready("l" if s else "f0")
        if s == 0:
            matmul(f_v.at[0], wv.at[s, j], acc.at[j], kb, rb)
        else:
            matmul(l_v.at[0], wv.at[s, j], acc2.at[j], kb, rb, init=False)
        full = acc2 if s else acc

        def fn(at):
            for zz in range(Z):
                ps_s[s, j, zz, at(), :] = full[j, at((zz * 2 + 1 - k) * b), :].astype(BF)

        pieces(b, fn)
        send(ps_s.at[s, j], ps_r.at[s, j], pa_s.at[s, j], pa_r.at[s, j], partner)

    def f1(j):
        ready("f1")

        matmul(f_v.at[1], wv.at[0, j], acc2.at[j], kb, rb)

    def pair(s, j):
        arrived(ps_r.at[s, j], pa_s.at[s, j], pa_r.at[s, j])

    def s1(j, q):
        at0 = (q * 2 + k) * b
        keep = jnp.where(z == q, 1.0, 0.0)

        @pl.when(jnp.logical_not(edge))
        def _():
            arrived(zi_r.at[0, j, q], io_s.at[j, q], io_r.at[0, j, q])

            def fn(at):
                acc[j, at(at0), :] += zi_r[0, j, q, at(), :].astype(F32)

            pieces(b, fn)

        def fn(at):
            value = acc[j, at(at0), :] + ps_r[0, j, q, at(), :].astype(F32)
            value = value - keep * m_v[1, at(), j * n:(j + 1) * n]
            acc[j, at(at0), :] = value
            zs_s[0, j, q, at(), :] = value.astype(BF)

        pieces(b, fn)
        send(zs_s.at[0, j, q], zi_r.at[mid_slot, j, q],
             io_s.at[j, q], io_r.at[mid_slot, j, q], inward)

    def s2(j, q):
        at = rows(q * 2 + k, b)
        blk = xg.at[1, j, at, :]

        @pl.when(mid)
        def _():
            arrived(zi_r.at[1, j, q], io_s.at[j, q], io_r.at[1, j, q])

            def fn(piece):
                at0 = (q * 2 + k) * b
                total = acc[j, piece(at0), :] + zi_r[1, j, q, piece(), :].astype(F32)
                xg[1, j, piece(at0), :] = (-total).astype(BF)

            pieces(b, fn)

        @pl.when(jnp.logical_not(mid))
        def _():
            arrived(blk, t_s.at[j, q], t_r.at[j, q])

        @pl.when(jnp.logical_not(edge))
        def _():
            send(blk, blk, t_s.at[j, q], t_r.at[j, q], outward, False)

        send(blk, blk, xp_s.at[1, j, q], xp_r.at[1, j, q], partner)

    def p5(j):
        pair(1, j)
        for d in range(1, Z):
            zz = zz_of(d)

            def fn(at):
                value = acc2[j, at((zz * 2 + k) * b), :] + ps_r[1, j, zz, at(), :].astype(F32)
                zs_s[1, j, zz, at(), :] = value.astype(BF)

            pieces(b, fn)
            send(zs_s.at[1, j, zz], zs_r.at[j, z],
                 za_s.at[j, d], za_r.at[j, z], zpeer(zz))

    def p6(j):
        for d in range(1, Z):
            zz = zz_of(d)
            arrived(zs_r.at[j, zz], za_s.at[j, d], za_r.at[j, zz])

        def fn(at):
            total = acc2[j, at(c * b), :] + ps_r[1, j, z, at(), :].astype(F32)
            for d in range(1, Z):
                total = total + zs_r[j, zz_of(d), at(), :].astype(F32)
            cols = slice(j * n, (j + 1) * n)
            tr_v[at(), cols] = m_v[2, at(), cols] - total

        pieces(b, fn)

    h = e // R // 2

    def gram(s):
        for j in range(CHUNKS):
            cols = slice(j * n, (j + 1) * n)
            block = min(256, rb)
            if s == 0:
                pacc[:, cols] = jnp.zeros((e, n), F32)

            def step(q, carry):
                at = pl.ds(pl.multiple_of(q * block, block), block)
                pacc[:, cols] += lax.dot_general(
                    wv[s, 0, at, :], wv[s, j, at, :], (((0,), (0,)), ((), ())),
                    preferred_element_type=F32)
                return carry

            lax.fori_loop(0, rb // block, step, 0)

    def q0():
        gram(1)
        send(pacc.at[rows(r * 2 + 1 - k, h), :], pp_r, q_s.at[0], q_r.at[0], partner)

    def q1():
        arrived(pp_r, q_s.at[0], q_r.at[0])
        pz[z] = pacc[rows(r * 2 + k, h), :] + pp_r[...]
        for d in range(1, Z):
            send(pz.at[z], pz.at[z], qz_s.at[d], qz_r.at[z], zpeer(zz_of(d)))

    def q2():
        for d in range(1, Z):
            zz = zz_of(d)
            arrived(pz.at[zz], qz_s.at[d], qz_r.at[zz])
        total = pz[0]
        for zz in range(1, Z):
            total = total + pz[zz]
        pg[k, r] = total
        mine = pg.at[k, r]
        for d in range(1, R):
            send(mine, mine, qr_s.at[d], qr_r.at[r], (rr_of(d), c))

    def q3():
        for d in range(1, R):
            rr = rr_of(d)
            arrived(pg.at[k, rr], qr_s.at[d], qr_r.at[rr])
        send(pg.at[k], pg.at[k], q_s.at[1], q_r.at[1], partner)

    def q4():
        arrived(pg.at[1 - k], q_s.at[1], q_r.at[1])
        for kk in range(2):
            copy = pltpu.make_async_copy(pg.at[kk], pr_out.at[:, kk], po_sem.at[kk])
            copy.start()
            local.append(copy)

    def full4(s, j):
        p4_wait(s, j)
        p4(s, j)

    A, B = 0, 1
    ready("m")
    half = (Z + 1) // 2
    p0(A)
    p1(0, A)
    p0(B)
    p2(0, A)
    p3(0, A)
    p1(0, B)
    p2(0, B)
    full4(0, A)
    pair(0, A)
    s1(A, 0)
    f1(A)
    p3(0, B)
    for q in range(1, Z - 1):
        s1(A, q)
    full4(0, B)
    s1(A, Z - 1)
    for q in range(half):
        s2(A, q)
    pair(0, B)
    s1(B, 0)
    for q in range(half, Z):
        s2(A, q)
    s1(B, 1)
    p2(1, A)
    for q in range(2, Z):
        s1(B, q)
    s2(B, 0)
    p3(1, A)
    for q in range(1, Z):
        s2(B, q)
    f1(B)
    full4(1, A)
    p2(1, B)
    p5(A)
    gram(0)
    p3(1, B)
    p4_wait(1, B)
    q0()
    p4(1, B)
    q1()
    p6(A)
    p5(B)
    q2()
    q3()
    p6(B)
    copy = pltpu.make_async_copy(tr_v, tr_out.at[0], po_sem.at[2])
    copy.start()
    local.append(copy)
    q4()
    for copy in sends:
        copy.wait_send()

    @pl.when(jnp.logical_not(edge))
    def _():
        for j in range(CHUNKS):
            for q in range(Z):
                blk = xg.at[1, j, rows(q * 2 + k, b), :]
                pltpu.make_async_remote_copy(
                    src_ref=blk, dst_ref=blk, send_sem=t_s.at[j, q], recv_sem=t_r.at[j, q],
                    device_id=outward, device_id_type=MESH,
                ).wait_send()

    for copy in local:
        copy.wait()


def hand_over(*refs):
    count = len(refs) // 2
    sems = refs[-1]
    copies = [
        pltpu.make_async_copy(refs[i], refs[count + i], sems.at[i]) for i in range(count)
    ]
    for copy in copies:
        copy.start()
    for copy in copies:
        copy.wait()


def body(R, Z, m, p, f, l):
    b, cols = m.shape[1], m.shape[2]
    n = cols // CHUNKS
    e = cols // 2
    rb, kb = R * b, 2 * Z * b
    h = e // R // 2
    sem = pltpu.SemaphoreType.DMA
    V = pltpu.VMEM
    flops = 2 * 5 * rb * kb * cols
    any_spec = pl.BlockSpec(memory_space=pl.ANY)
    whitened, trailing, proj = pl.pallas_call(
        functools.partial(kernel, R, Z, b, n, e),
        out_shape=(
            jax.ShapeDtypeStruct((2, rb, cols), BF),
            jax.ShapeDtypeStruct((1, b, cols), F32),
            jax.ShapeDtypeStruct((R, 2, h, cols), F32),
        ),
        in_specs=[any_spec] * 4,
        out_specs=(any_spec,) * 3,
        scratch_shapes=[
            V(m.shape, F32), V(p.shape, BF), V(f.shape, BF), V(l.shape, BF),
            V((2, CHUNKS, kb, n), BF),
            V((2, CHUNKS, rb, n), BF), V((2, CHUNKS, R, b, n), BF),
            V((2, CHUNKS, rb, n), BF),
            V((CHUNKS, kb, n), F32), V((CHUNKS, kb, n), F32),
            V((2, CHUNKS, Z, b, n), BF), V((2, CHUNKS, Z, b, n), BF),
            V((2, CHUNKS, Z, b, n), BF), V((CHUNKS, Z, b, n), BF),
            V((b, cols), F32),
            V((e, cols), F32), V((h, cols), F32), V((Z, h, cols), F32),
            V((2, R, h, cols), F32), V((2, CHUNKS, Z, b, n), BF),
            sem((6,)), sem((2, CHUNKS)), sem((3,)),
            sem((2, CHUNKS, Z)), sem((2, CHUNKS, Z)),
            sem((2, CHUNKS, Z)), sem((2, CHUNKS, Z)),
            sem((2, CHUNKS, R)), sem((2, CHUNKS, R)),
            sem((2, CHUNKS, R)), sem((2, CHUNKS, R)),
            sem((2, CHUNKS)), sem((2, CHUNKS)),
            sem((CHUNKS, Z)), sem((CHUNKS, Z)),
            sem((2,)), sem((2,)), sem((Z,)), sem((Z,)), sem((R,)), sem((R,)),
            sem((CHUNKS, Z)), sem((2, CHUNKS, Z)), sem((CHUNKS, Z)), sem((CHUNKS, Z)),
        ],
        compiler_params=pltpu.CompilerParams(
            collective_id=0, has_side_effects=True, vmem_limit_bytes=60 * 2**20),
        cost_estimate=pl.CostEstimate(
            flops=flops, bytes_accessed=10 * rb * kb, transcendentals=0),
    )(m, p, f, l)
    results = (whitened, trailing, proj.reshape(e, cols))
    return pl.pallas_call(
        hand_over,
        out_shape=tuple(jax.ShapeDtypeStruct(a.shape, a.dtype) for a in results),
        in_specs=[any_spec] * 3,
        out_specs=(any_spec,) * 3,
        scratch_shapes=[sem((3,))],
    )(*results)


def solution(mesh):
    R, Z = mesh.shape["row"], mesh.shape["col"] // 2
    in_specs = (
        P(None, ("row", "col"), None),
        P(None, "col", "row"),
        P(None, "row", "col"),
        P(None, "row", "col"),
    )
    out_specs = (P(None, "col", None), P(None, ("row", "col"), None), P())
    return jax.shard_map(
        functools.partial(body, R, Z), mesh=mesh, in_specs=in_specs, out_specs=out_specs,
        check_vma=False,
    )
```

```python
import functools

import jax
import jax.numpy as jnp
from jax import lax
from jax.experimental import pallas as pl
from jax.experimental.pallas import tpu as pltpu
from jax.sharding import PartitionSpec as P

MESH = pl.DeviceIdType.MESH
BF = jnp.bfloat16
F32 = jnp.float32
CHUNKS = 2


def kernel(
    R, Z, b, n, e,
    m_h, p_h, f_h, l_h,
    wh_out, tr_out, pr_out,
    m_v, p_v, f_v, l_v, xg, rs_s, rs_r, wv, acc, acc2, ps_s, ps_r, zs_s, zs_r, tr_v,
    pacc, pp_r, pz, pg, zi_r,
    ld_sem, out_sem, po_sem,
    xz_s, xz_r, xp_s, xp_r, ra_s, ra_r, rb_s, rb_r, pa_s, pa_r, za_s, za_r,
    q_s, q_r, qz_s, qz_r, qr_s, qr_r, io_s, io_r, t_s, t_r,
):
    r = lax.axis_index("row")
    c = lax.axis_index("col")
    z = lax.div(c, 2)
    k = lax.rem(c, 2)
    rb, kb = R * b, 2 * Z * b
    partner = (r, z * 2 + 1 - k)

    def zpeer(zz):
        return (r, zz * 2 + k)

    left = z < Z // 2
    edge = (z == 0) | (z == Z - 1)
    mid = (z == Z // 2 - 1) | (z == Z // 2)
    mid_slot = jnp.where(mid, 1, 0)
    inward = zpeer(jnp.where(left, z + 1, z - 1))
    outward = zpeer(jnp.where(left, jnp.maximum(z - 1, 0), jnp.minimum(z + 1, Z - 1)))

    def zz_of(d):
        return lax.rem(z + d, Z)

    def rr_of(d):
        return lax.rem(r + d, R)

    def rows(block, size, count=None):
        return pl.ds(pl.multiple_of(block * size, size), size if count is None else count)

    loads = {}

    def load(name, index, src, dst):
        copy = pltpu.make_async_copy(src, dst, ld_sem.at[index])
        copy.start()
        loads[name] = copy

    load("m", 0, m_h, m_v)
    load("p0", 1, p_h.at[0], p_v.at[0])
    load("f0", 2, f_h.at[0], f_v.at[0])
    load("p1", 3, p_h.at[1], p_v.at[1])
    load("f1", 4, f_h.at[1], f_v.at[1])
    load("l", 5, l_h.at[0], l_v.at[0])

    barrier = pltpu.get_barrier_semaphore()
    peers = [partner] + [zpeer(zz_of(d)) for d in range(1, Z)]
    peers += [(rr_of(d), c) for d in range(1, R)]
    for peer in peers:
        pl.semaphore_signal(barrier, inc=1, device_id=peer, device_id_type=MESH)
    pl.semaphore_wait(barrier, len(peers))

    sends = []
    local = []

    def send(src, dst, ssem, rsem, device, into=None):
        copy = pltpu.make_async_remote_copy(
            src_ref=src, dst_ref=dst, send_sem=ssem, recv_sem=rsem,
            device_id=device, device_id_type=MESH,
        )
        copy.start()
        if into is None:
            sends.append(copy)

    def arrived(dst, ssem, rsem):
        pltpu.make_async_remote_copy(
            src_ref=dst, dst_ref=dst, send_sem=ssem, recv_sem=rsem,
            device_id=partner, device_id_type=MESH,
        ).wait_recv()

    waited = set()

    def ready(name):
        if name not in waited:
            waited.add(name)
            loads[name].wait()

    def matmul(a, x, total, put):
        tile = min(1024, total)

        def step(i, carry):
            at = pl.ds(pl.multiple_of(i * tile, tile), tile)
            put(at, jnp.dot(a[at, :], x[...], preferred_element_type=F32))
            return carry

        lax.fori_loop(0, total // tile, step, 0)

    def xblock(s, j, cc):
        return xg.at[s, j, rows(cc, b), :]

    def give_x(s, j):
        mine = xblock(s, j, c)
        for d in range(1, Z):
            send(mine, mine, xz_s.at[s, j, d], xz_r.at[s, j, z], zpeer(zz_of(d)))
        send(mine, mine, xp_s.at[s, j, z], xp_r.at[s, j, z], partner)

    def p0(j):
        xg[0, j, rows(c, b), :] = m_v[0, :, j * n:(j + 1) * n].astype(BF)
        give_x(0, j)

    def p1(s, j):
        for d in range(1, Z):
            zz = zz_of(d)
            blk = xblock(s, j, zz * 2 + k)
            arrived(blk, xz_s.at[s, j, d], xz_r.at[s, j, zz])
            send(blk, blk, xp_s.at[s, j, zz], xp_r.at[s, j, zz], partner)

    def p2(s, j):
        for d in range(Z):
            zz = zz_of(d)
            arrived(xblock(s, j, zz * 2 + 1 - k), xp_s.at[s, j, zz], xp_r.at[s, j, zz])
        ready("p%d" % s)

        def put(at, value):
            acc[j, at, :] = value
            rs_s[s, j, at, :] = value.astype(BF)

        matmul(p_v.at[s], xg.at[s, j], rb, put)
        for d in range(1, R):
            rr = rr_of(d)
            send(rs_s.at[s, j, rows(rr, b), :], rs_r.at[s, j, r],
                 ra_s.at[s, j, d], ra_r.at[s, j, r], (rr, c))

    def p3(s, j):
        total = acc[j, rows(r, b), :]
        for d in range(1, R):
            rr = rr_of(d)
            arrived(rs_r.at[s, j, rr], ra_s.at[s, j, d], ra_r.at[s, j, rr])
            total = total + rs_r[s, j, rr].astype(F32)
        wv[s, j, rows(r, b), :] = total.astype(BF)
        mine = wv.at[s, j, rows(r, b), :]
        for d in range(1, R):
            send(mine, mine, rb_s.at[s, j, d], rb_r.at[s, j, r], (rr_of(d), c))

    def p4_wait(s, j):
        for d in range(1, R):
            rr = rr_of(d)
            arrived(wv.at[s, j, rows(rr, b), :], rb_s.at[s, j, d], rb_r.at[s, j, rr])
        copy = pltpu.make_async_copy(
            wv.at[s, j], wh_out.at[s, :, pl.ds(j * n, n)], out_sem.at[s, j])
        copy.start()
        local.append(copy)

    def p4(s, j):
        if s == 0:
            ready("f0")

            def put(at, value):
                acc[j, at, :] = value

            matmul(f_v.at[0], wv.at[s, j], kb, put)
        else:
            ready("l")

            def put(at, value):
                acc[j, at, :] = acc2[j, at, :] + value

            matmul(l_v.at[0], wv.at[s, j], kb, put)
        for zz in range(Z):
            ps_s[s, j, zz] = acc[j, rows(zz * 2 + 1 - k, b), :].astype(BF)
        send(ps_s.at[s, j], ps_r.at[s, j], pa_s.at[s, j], pa_r.at[s, j], partner)

    def f1(j):
        ready("f1")

        def put(at, value):
            acc2[j, at, :] = value

        matmul(f_v.at[1], wv.at[0, j], kb, put)

    def pair(s, j):
        arrived(ps_r.at[s, j], pa_s.at[s, j], pa_r.at[s, j])

    def s1(j, q):
        at = rows(q * 2 + k, b)
        own = jnp.where(z == q, m_v[1, :, j * n:(j + 1) * n], 0.0)
        acc[j, at, :] = acc[j, at, :] + ps_r[0, j, q].astype(F32) - own

        @pl.when(jnp.logical_not(edge))
        def _():
            arrived(zi_r.at[0, j, q], io_s.at[j, q], io_r.at[0, j, q])
            acc[j, at, :] = acc[j, at, :] + zi_r[0, j, q].astype(F32)

        zs_s[0, j, q] = acc[j, at, :].astype(BF)
        send(zs_s.at[0, j, q], zi_r.at[mid_slot, j, q],
             io_s.at[j, q], io_r.at[mid_slot, j, q], inward)

    def s2(j, q):
        at = rows(q * 2 + k, b)
        blk = xg.at[1, j, at, :]

        @pl.when(mid)
        def _():
            arrived(zi_r.at[1, j, q], io_s.at[j, q], io_r.at[1, j, q])
            xg[1, j, at, :] = (-(acc[j, at, :] + zi_r[1, j, q].astype(F32))).astype(BF)

        @pl.when(jnp.logical_not(mid))
        def _():
            arrived(blk, t_s.at[j, q], t_r.at[j, q])

        @pl.when(jnp.logical_not(edge))
        def _():
            send(blk, blk, t_s.at[j, q], t_r.at[j, q], outward, False)

        send(blk, blk, xp_s.at[1, j, q], xp_r.at[1, j, q], partner)

    def p5(j):
        pair(1, j)
        for d in range(1, Z):
            zz = zz_of(d)
            value = acc[j, rows(zz * 2 + k, b), :] + ps_r[1, j, zz].astype(F32)
            zs_s[1, j, zz] = value.astype(BF)
            send(zs_s.at[1, j, zz], zs_r.at[j, z],
                 za_s.at[j, d], za_r.at[j, z], zpeer(zz))

    def p6(j):
        total = acc[j, rows(c, b), :] + ps_r[1, j, z].astype(F32)
        for d in range(1, Z):
            zz = zz_of(d)
            arrived(zs_r.at[j, zz], za_s.at[j, d], za_r.at[j, zz])
            total = total + zs_r[j, zz].astype(F32)
        tr_v[:, j * n:(j + 1) * n] = m_v[2, :, j * n:(j + 1) * n] - total

    h = e // R // 2

    def gram(s):
        for j in range(CHUNKS):
            value = lax.dot_general(
                wv[s, 0], wv[s, j], (((0,), (0,)), ((), ())), preferred_element_type=F32)
            at = slice(j * n, (j + 1) * n)
            if s == 0:
                pacc[:, at] = value
            else:
                pacc[:, at] = pacc[:, at] + value

    def q0():
        gram(1)
        send(pacc.at[rows(r * 2 + 1 - k, h), :], pp_r, q_s.at[0], q_r.at[0], partner)

    def q1():
        arrived(pp_r, q_s.at[0], q_r.at[0])
        pz[z] = pacc[rows(r * 2 + k, h), :] + pp_r[...]
        for d in range(1, Z):
            send(pz.at[z], pz.at[z], qz_s.at[d], qz_r.at[z], zpeer(zz_of(d)))

    def q2():
        for d in range(1, Z):
            zz = zz_of(d)
            arrived(pz.at[zz], qz_s.at[d], qz_r.at[zz])
        total = pz[0]
        for zz in range(1, Z):
            total = total + pz[zz]
        pg[k, r] = total
        mine = pg.at[k, r]
        for d in range(1, R):
            send(mine, mine, qr_s.at[d], qr_r.at[r], (rr_of(d), c))

    def q3():
        for d in range(1, R):
            rr = rr_of(d)
            arrived(pg.at[k, rr], qr_s.at[d], qr_r.at[rr])
        send(pg.at[k], pg.at[k], q_s.at[1], q_r.at[1], partner)

    def q4():
        arrived(pg.at[1 - k], q_s.at[1], q_r.at[1])
        for kk in range(2):
            copy = pltpu.make_async_copy(pg.at[kk], pr_out.at[:, kk], po_sem.at[kk])
            copy.start()
            local.append(copy)

    def full4(s, j):
        p4_wait(s, j)
        p4(s, j)

    A, B = 0, 1
    ready("m")
    half = (Z + 1) // 2
    p0(A)
    p1(0, A)
    p0(B)
    p2(0, A)
    p3(0, A)
    p1(0, B)
    p2(0, B)
    full4(0, A)
    pair(0, A)
    s1(A, 0)
    f1(A)
    p3(0, B)
    for q in range(1, Z - 1):
        s1(A, q)
    full4(0, B)
    s1(A, Z - 1)
    for q in range(half):
        s2(A, q)
    pair(0, B)
    s1(B, 0)
    for q in range(half, Z):
        s2(A, q)
    s1(B, 1)
    p2(1, A)
    for q in range(2, Z):
        s1(B, q)
    s2(B, 0)
    p3(1, A)
    for q in range(1, Z):
        s2(B, q)
    f1(B)
    full4(1, A)
    p2(1, B)
    p5(A)
    gram(0)
    p3(1, B)
    p4_wait(1, B)
    q0()
    p4(1, B)
    q1()
    p6(A)
    p5(B)
    q2()
    q3()
    p6(B)
    copy = pltpu.make_async_copy(tr_v, tr_out.at[0], po_sem.at[2])
    copy.start()
    local.append(copy)
    q4()
    for copy in sends:
        copy.wait_send()

    @pl.when(jnp.logical_not(edge))
    def _():
        for j in range(CHUNKS):
            for q in range(Z):
                blk = xg.at[1, j, rows(q * 2 + k, b), :]
                pltpu.make_async_remote_copy(
                    src_ref=blk, dst_ref=blk, send_sem=t_s.at[j, q], recv_sem=t_r.at[j, q],
                    device_id=outward, device_id_type=MESH,
                ).wait_send()

    for copy in local:
        copy.wait()


def body(R, Z, m, p, f, l):
    b, cols = m.shape[1], m.shape[2]
    n = cols // CHUNKS
    e = cols // 2
    rb, kb = R * b, 2 * Z * b
    h = e // R // 2
    sem = pltpu.SemaphoreType.DMA
    V = pltpu.VMEM
    flops = 2 * 5 * rb * kb * cols
    any_spec = pl.BlockSpec(memory_space=pl.ANY)
    whitened, trailing, proj = pl.pallas_call(
        functools.partial(kernel, R, Z, b, n, e),
        out_shape=(
            jax.ShapeDtypeStruct((2, rb, cols), BF),
            jax.ShapeDtypeStruct((1, b, cols), F32),
            jax.ShapeDtypeStruct((R, 2, h, cols), F32),
        ),
        in_specs=[any_spec] * 4,
        out_specs=(any_spec,) * 3,
        scratch_shapes=[
            V(m.shape, F32), V(p.shape, BF), V(f.shape, BF), V(l.shape, BF),
            V((2, CHUNKS, kb, n), BF),
            V((2, CHUNKS, rb, n), BF), V((2, CHUNKS, R, b, n), BF),
            V((2, CHUNKS, rb, n), BF),
            V((CHUNKS, kb, n), F32), V((CHUNKS, kb, n), F32),
            V((2, CHUNKS, Z, b, n), BF), V((2, CHUNKS, Z, b, n), BF),
            V((2, CHUNKS, Z, b, n), BF), V((CHUNKS, Z, b, n), BF),
            V((b, cols), F32),
            V((e, cols), F32), V((h, cols), F32), V((Z, h, cols), F32),
            V((2, R, h, cols), F32), V((2, CHUNKS, Z, b, n), BF),
            sem((6,)), sem((2, CHUNKS)), sem((3,)),
            sem((2, CHUNKS, Z)), sem((2, CHUNKS, Z)),
            sem((2, CHUNKS, Z)), sem((2, CHUNKS, Z)),
            sem((2, CHUNKS, R)), sem((2, CHUNKS, R)),
            sem((2, CHUNKS, R)), sem((2, CHUNKS, R)),
            sem((2, CHUNKS)), sem((2, CHUNKS)),
            sem((CHUNKS, Z)), sem((CHUNKS, Z)),
            sem((2,)), sem((2,)), sem((Z,)), sem((Z,)), sem((R,)), sem((R,)),
            sem((CHUNKS, Z)), sem((2, CHUNKS, Z)), sem((CHUNKS, Z)), sem((CHUNKS, Z)),
        ],
        compiler_params=pltpu.CompilerParams(
            collective_id=0, has_side_effects=True, vmem_limit_bytes=60 * 2**20),
        cost_estimate=pl.CostEstimate(
            flops=flops, bytes_accessed=10 * rb * kb, transcendentals=0),
    )(m, p, f, l)
    return whitened, trailing, proj.reshape(e, cols)


def solution(mesh):
    R, Z = mesh.shape["row"], mesh.shape["col"] // 2
    in_specs = (
        P(None, ("row", "col"), None),
        P(None, "col", "row"),
        P(None, "row", "col"),
        P(None, "row", "col"),
    )
    out_specs = (P(None, "col", None), P(None, ("row", "col"), None), P())
    return jax.shard_map(
        functools.partial(body, R, Z), mesh=mesh, in_specs=in_specs, out_specs=out_specs,
        check_vma=False,
    )
```
